32 devices in a mesh: groups: 2 (over x), space: 16 (over z, y, core).
Axes of the slice: x: 2, y: 2, z: 4, core: 2. Of those that a mesh axis runs over, the one named last changes fastest.
Arguments:
- node_latent: bfloat16 [12288, 512], P(('groups', 'space')), parts along dimension 0, may hold values from -6 to 6
- edge_latent: bfloat16 [65536, 512], P(('groups', 'space')), parts along dimension 0, may hold values from -6 to 6
- sender_local: int32 [32768], P('space'), may hold values from 0 to 383
- receiver_target: int32 [32768], P('space'), may hold values from 0 to 639, as said below
- row_list: int32 [16, 16, 16], P('space'), may hold values from 0 to 383
- edge_count: int32 [16], P('space'), may hold values from 1 to 2048, 16384 in all
- edge_in: bfloat16 [1536, 512], replicated, may hold values from -0.15625 to 0.15625
- edge_out: bfloat16 [512, 512], replicated, may hold values from -0.25 to 0.25
- node_in: bfloat16 [1024, 512], replicated, may hold values from -0.1875 to 0.1875
- node_out: bfloat16 [512, 512], replicated, may hold values from -0.25 to 0.25
Outputs:
- new_nodes: bfloat16 [12288, 512], P(('groups', 'space')), parts along dimension 0
- new_edges: bfloat16 [65536, 512], P(('groups', 'space')), parts along dimension 0
The draws below stay inside these ranges and needn't reach their ends.
There are 2 independent parts, one for each index of `groups`. The reference program is written for one: setup_inputs(seed, part) draws one part's arguments, and reference() takes and returns one part's arrays. A program takes and returns all parts, laid end to end along the dimension named above; an argument that names none is the same for every part. Nothing has to cross between parts.
Inputs may be any that keep to these rules, and one draw needn't show every extreme that they name: `receiver_target`: an entry below 384 names a node of the slot's own device; an entry t of 384 or more names slot (t - 384) % 16 of device (t - 384) // 16, never the slot's own device.
All inputs are finite; a program needn't handle non-finite values. No bound on the sum of `edge_count` on one device may be relied on, other than what follows from the above.
Results may differ from the reference program's by a relative error of at most 0.0052.
Values may be sent and summed in bfloat16 or wider, within the bound.
A program may use at most 64 MiB of HBM per device.

```python
import math
import jax
import jax.numpy as jnp
import numpy as np
from jax import lax

D = 512
NODE_DEV = 384
EDGE_DEV = 2048
CAP = 16
NODES = 6144
EDGES = 32768
N_SPACE = 16


def draw_receiver_target(key, part):
    key = jax.random.fold_in(key, 7)
    keys = jax.random.split(key, 4)
    part_total = EDGES // EDGE_DEV
    positions = jnp.arange(EDGES, dtype=jnp.int32)
    edge_owner = positions // EDGE_DEV
    choose_local = jax.random.randint(keys[0], (EDGES,), 0, 4)
    local_node = jax.random.randint(keys[1], (EDGES,), 0, NODE_DEV)
    offset = jax.random.randint(keys[2], (EDGES,), 1, part_total)
    slot_index = jax.random.randint(keys[3], (EDGES,), 0, CAP)
    partner = (edge_owner + offset) % part_total
    remote = NODE_DEV + partner * CAP + slot_index
    result = jnp.where(choose_local < 3, local_node, remote).astype(jnp.int32)
    return result.at[0].set(NODE_DEV + part_total * CAP - 1)


def set_ends(drawn, stream_key, least, largest):
    shape = drawn.shape
    spot = [jax.random.randint(jax.random.fold_in(stream_key, axis), (), 0, shape[axis]) for axis in range(len(shape))]
    drawn = drawn.at[tuple(spot)].set(least)
    longest = shape.index(max(shape))
    spot[longest] = (spot[longest] + 1) % shape[longest]
    return drawn.at[tuple(spot)].set(largest)


def block_levels(key, dims, cuts, low, top_value):
    factor_of = 1.0
    for dim, blocks in cuts:
        heights = jax.random.uniform(jax.random.fold_in(jax.random.fold_in(key, 6), dim), (blocks,), jnp.float32, low / len(cuts), top_value / len(cuts))
        factor_of = factor_of * jnp.repeat(jnp.exp(heights), dims[dim] // blocks).reshape((-1,) + (1,) * (len(dims) - 1 - dim))
    return factor_of


def length_profile(number_of, total, reach, slope):
    loads = [(1 << 20) // math.isqrt(grade ** slope) + 1 for grade in range(2, number_of + 1)]
    rest, given = total - reach - (number_of - 1), [1] * (number_of - 1)
    while rest > 0:
        candidates = [i for i in range(number_of - 1) if given[i] < reach]
        pool, remaining = sum([loads[i] for i in candidates]), rest
        for i in candidates:
            extra = min(reach - given[i], max(1, remaining * loads[i] // pool), rest)
            given[i] = given[i] + extra
            rest = rest - extra
    return np.array([reach] + given)


def ragged(own_key, count, total, limit, lean):
    if count == 2:
        one = jax.random.randint(own_key, (), max(1, total - limit), min(limit, total - 1) + 1)
        return jnp.stack([one, total - one])
    sizes = jnp.asarray(length_profile(count, total, limit, lean), jnp.int32)
    couples = (count - 1) // 2
    source_of, receiver = sizes[1:1 + 2 * couples:2], sizes[2:2 + 2 * couples:2]
    slack = jnp.minimum(source_of - 1, limit - receiver)
    shifted = jax.random.randint(jax.random.fold_in(own_key, 1), (couples,), 0, 1 << 20) % (slack + 1)
    sizes = sizes.at[1:1 + 2 * couples:2].set(source_of - shifted).at[2:2 + 2 * couples:2].set(receiver + shifted)
    return sizes[jax.random.permutation(jax.random.fold_in(own_key, 2), count)]


def bell_draw(rng, extent, scale, bound, cuts=(), kind=jnp.bfloat16):
    gain = block_levels(rng, extent, cuts, -0.22, 0.18) if cuts else 1.0
    entries = jax.random.normal(rng, extent, jnp.float32) * scale * gain
    return jnp.minimum(jnp.maximum(entries, -bound), bound).astype(kind)


def setup_inputs(seed: int = 0, part: int = 0) -> dict:
    streams_of = jax.random.split(jax.random.key(seed), 11)
    own_keys = jax.random.split(jax.random.fold_in(streams_of[10], part), 11)
    return {
        "node_latent": bell_draw(own_keys[0], (NODES, D), 1.0, 6.0, ((0, 16),)),
        "edge_latent": bell_draw(own_keys[1], (EDGES, D), 1.0, 6.0, ((0, 16),)),
        "sender_local": set_ends(jax.random.randint(streams_of[2], (EDGES,), 0, NODE_DEV), jax.random.fold_in(streams_of[2], 1), 0, NODE_DEV - 1).astype(jnp.int32),
        "receiver_target": draw_receiver_target(jax.random.fold_in(streams_of[10], 71), part),
        "row_list": set_ends(jax.random.randint(streams_of[4], (N_SPACE, N_SPACE, CAP), 0, NODE_DEV), jax.random.fold_in(streams_of[4], 1), 0, NODE_DEV - 1).astype(jnp.int32),
        "edge_count": ragged(streams_of[5], N_SPACE, N_SPACE * EDGE_DEV // 2, EDGE_DEV, 2).astype(jnp.int32),
        "edge_in": bell_draw(streams_of[6], (3 * D, D), (3 * D) ** -0.5, 0.15625),
        "edge_out": bell_draw(streams_of[7], (D, D), D ** -0.5, 0.25),
        "node_in": bell_draw(streams_of[8], (2 * D, D), (2 * D) ** -0.5, 0.1875),
        "node_out": bell_draw(streams_of[9], (D, D), D ** -0.5, 0.25),
    }


epsilon = 1e-05

def normalize(values):
    center = values - lax.optimization_barrier(jnp.mean(values, axis=-1, keepdims=True))
    spread = lax.optimization_barrier(jnp.mean(center * center, axis=-1, keepdims=True))
    return center * lax.rsqrt(spread + epsilon)

def finish_update(latent, first, second_weight):
    hidden = jax.nn.silu(first).astype(jnp.bfloat16)
    mixed_out = jnp.dot(hidden, second_weight, preferred_element_type=jnp.float32)
    return (latent.astype(jnp.float32) + normalize(mixed_out)).astype(jnp.bfloat16)

def reference(node_latent, edge_latent, sender_local, receiver_target, row_list, edge_count, edge_in, edge_out, node_in, node_out):
    positions = jnp.arange(EDGES, dtype=jnp.int32)
    edge_owner = positions // EDGE_DEV
    live_rows = positions % EDGE_DEV < edge_count[edge_owner]
    senders = edge_owner * NODE_DEV + sender_local
    remote_slot = jnp.maximum(receiver_target - NODE_DEV, 0)
    remote_part = remote_slot // CAP
    remote_node = remote_part * NODE_DEV + row_list[remote_part, edge_owner, remote_slot % CAP]
    receivers = jnp.where(receiver_target < NODE_DEV, edge_owner * NODE_DEV + receiver_target, remote_node).astype(jnp.int32)
    edge_first = jnp.dot(edge_latent, edge_in[:D], preferred_element_type=jnp.float32)
    edge_first = edge_first + jnp.dot(node_latent[senders], edge_in[D:2 * D], preferred_element_type=jnp.float32)
    edge_first = edge_first + jnp.dot(node_latent[receivers], edge_in[2 * D:], preferred_element_type=jnp.float32)
    updated = finish_update(edge_latent, edge_first, edge_out)
    new_edges = jnp.where(live_rows[:, None], updated, edge_latent)
    messages = jnp.where(live_rows[:, None], updated.astype(jnp.float32), jnp.zeros((), jnp.float32))
    aggregate = jax.ops.segment_sum(messages, receivers, num_segments=NODES)
    aggregate_half = aggregate.astype(jnp.bfloat16)
    node_first = jnp.dot(node_latent, node_in[:D], preferred_element_type=jnp.float32)
    node_first = node_first + jnp.dot(aggregate_half, node_in[D:], preferred_element_type=jnp.float32)
    new_nodes = finish_update(node_latent, node_first, node_out)
    return (new_nodes, new_edges)
```

```python
import functools

import jax
import jax.numpy as jnp
from jax import lax
from jax.experimental import pallas as pl
from jax.experimental.pallas import tpu as pltpu
from jax.sharding import PartitionSpec as P

epsilon = 1e-05
lanes = 128
block_rows = 256
MESH = pl.DeviceIdType.MESH
bf16 = jnp.bfloat16
f32 = jnp.float32


def dot(left, right):
    return jnp.dot(left, right, preferred_element_type=f32)


def iota(shape, axis):
    return lax.broadcasted_iota(jnp.int32, shape, axis)


def half_silu(first):
    half = 0.5 * first
    return (half + half * jnp.tanh(half)).astype(bf16)


def residual_norm(latent, mixed):
    center = mixed - jnp.mean(mixed, axis=-1, keepdims=True)
    spread = jnp.mean(center * center, axis=-1, keepdims=True)
    return latent.astype(f32) + center * lax.rsqrt(spread + epsilon)


def kernel(
    peers,
    pad,
    count_ref,
    node_hbm,
    edge_hbm,
    send_hbm,
    recv_hbm,
    list_hbm,
    edge_in_hbm,
    edge_out_hbm,
    node_in_hbm,
    node_out_hbm,
    new_nodes_hbm,
    new_edges_hbm,
    node_v,
    edge_v,
    send_v,
    recv_v,
    list_v,
    table_v,
    ends_v,
    edge_out_v,
    node_in_v,
    node_out_v,
    first_v,
    far_hot_v,
    spread_v,
    back_v,
    new_nodes_v,
    new_edges_v,
    out_rows,
    in_rows,
    out_sums,
    in_sums,
    load_sem,
    store_sem,
    sems,
):
    node_dev, width = node_v.shape
    edge_dev = edge_v.shape[0]
    slots = peers * pad
    near = width + 2 * node_dev
    blocks = edge_dev // block_rows
    parts = block_rows // lanes
    me = lax.axis_index("space")

    barrier = pltpu.get_barrier_semaphore()

    def greet(k, carry):
        peer = lax.rem(me + k, peers)
        pl.semaphore_signal(barrier, inc=1, device_id={"space": peer}, device_id_type=MESH)
        return carry

    lax.fori_loop(1, peers, greet, 0)

    loads = [
        pltpu.make_async_copy(source, target, load_sem.at[number])
        for number, (source, target) in enumerate(
            [
                (list_hbm, list_v),
                (node_hbm, node_v),
                (edge_in_hbm.at[pl.ds(width, 2 * width)], ends_v),
                (send_hbm, send_v),
                (recv_hbm, recv_v),
                (edge_in_hbm.at[pl.ds(0, width)], table_v.at[pl.ds(0, width)]),
                (edge_hbm, edge_v),
                (edge_out_hbm, edge_out_v),
                (node_in_hbm, node_in_v),
                (node_out_hbm, node_out_v),
            ]
        )
    ]
    for load in loads:
        load.start()

    own = pl.ds(pl.multiple_of(me * pad, pad), pad)
    in_rows[own, :] = jnp.zeros((pad, width), bf16)
    in_sums[own, :] = jnp.zeros((pad, width), bf16)

    loads[0].wait()
    listed = list_v[...]
    rows = jnp.concatenate(
        [jnp.broadcast_to(listed[p : p + 1], (pad, pad)) for p in range(peers)], axis=0
    ).astype(f32)
    picked = lax.rem(iota((slots, pad), 0), pad) == iota((slots, pad), 1)
    column = jnp.sum(jnp.where(picked, rows, 0.0), axis=1, keepdims=True)
    wanted = (column.astype(jnp.int32) == iota((slots, node_dev), 1)).astype(f32)
    loads[1].wait()
    out_rows[...] = dot(wanted.astype(bf16), node_v[...]).astype(bf16)

    def transfer(source, target, number, peer):
        theirs = pl.ds(pl.multiple_of(peer * pad, pad), pad)
        return pltpu.make_async_remote_copy(
            src_ref=source.at[theirs],
            dst_ref=target.at[own],
            send_sem=sems.at[number, peer],
            recv_sem=sems.at[number + 1, me],
            device_id={"space": peer},
            device_id_type=MESH,
        )

    def arrival(source, target, number, peer):
        theirs = pl.ds(pl.multiple_of(peer * pad, pad), pad)
        return pltpu.make_async_remote_copy(
            src_ref=source.at[theirs],
            dst_ref=target.at[theirs],
            send_sem=sems.at[number, peer],
            recv_sem=sems.at[number + 1, peer],
            device_id={"space": peer},
            device_id_type=MESH,
        )

    def each_peer(action):
        def step(k, carry):
            action(lax.rem(me + k, peers))
            return carry

        lax.fori_loop(1, peers, step, 0)

    pl.semaphore_wait(barrier, peers - 1)
    each_peer(lambda peer: transfer(out_rows, in_rows, 0, peer).start())

    back_v[...] = wanted.T.astype(bf16)
    loads[2].wait()
    table_v[pl.ds(width, node_dev), :] = dot(node_v[...], ends_v[pl.ds(0, width), :]).astype(bf16)
    table_v[pl.ds(width + node_dev, node_dev), :] = dot(
        node_v[...], ends_v[pl.ds(width, width), :]
    ).astype(bf16)
    for load in loads[3:]:
        load.wait()
    live_count = count_ref[0]

    def columns_of(index_ref, block):
        return jnp.concatenate(
            [
                jnp.broadcast_to(index_ref[pl.ds(block * parts + j, 1), :], (lanes, lanes)).T
                for j in range(parts)
            ],
            axis=0,
        )

    lane_ids = iota((block_rows, lanes), 1)

    def hot(columns, low, high):
        return jnp.concatenate(
            [(columns == lane_ids + c).astype(f32).astype(bf16) for c in range(low, high, lanes)],
            axis=1,
        )

    def before(block, carry):
        here = pl.ds(pl.multiple_of(block * block_rows, block_rows), block_rows)
        senders = columns_of(send_v, block)
        receivers = columns_of(recv_v, block)
        left = jnp.concatenate(
            [edge_v[here, :], hot(senders, 0, node_dev), hot(receivers, 0, node_dev)], axis=1
        )
        first_v[here, :] = dot(left, table_v[pl.ds(0, near), :])
        far_hot_v[here, :] = hot(receivers, node_dev, node_dev + slots)
        for j in range(parts):
            place = block * block_rows + j * lanes
            live = place + iota((1, lanes), 1) < live_count
            target = jnp.where(live, recv_v[pl.ds(block * parts + j, 1), :], -1)
            spread = target == iota((node_dev + slots, lanes), 0)
            spread_v[:, pl.ds(pl.multiple_of(place, lanes), lanes)] = spread.astype(f32).astype(
                bf16
            )
        return carry

    lax.fori_loop(0, blocks, before, 0)

    each_peer(lambda peer: arrival(out_rows, in_rows, 0, peer).wait_recv())
    table_v[pl.ds(near, slots), :] = dot(in_rows[...], ends_v[pl.ds(width, width), :]).astype(bf16)

    def store(block):
        here = pl.ds(pl.multiple_of(block * block_rows, block_rows), block_rows)
        return pltpu.make_async_copy(
            new_edges_v.at[here], new_edges_hbm.at[here], store_sem.at[block]
        )

    def after(block, carry):
        here = pl.ds(pl.multiple_of(block * block_rows, block_rows), block_rows)
        first = first_v[here, :] + dot(far_hot_v[here, :], table_v[pl.ds(near, slots), :])
        mixed = dot(half_silu(first), edge_out_v[...])
        old = edge_v[here, :]
        updated = residual_norm(old, mixed)
        live = block * block_rows + iota((block_rows, 1), 0) < live_count
        new_edges_v[here, :] = jnp.where(live, updated, old.astype(f32)).astype(bf16)
        store(block).start()
        return carry

    lax.fori_loop(0, blocks, after, 0)

    out_sums[...] = dot(spread_v[pl.ds(node_dev, slots), :], new_edges_v[...]).astype(bf16)
    each_peer(lambda peer: transfer(out_sums, in_sums, 2, peer).start())

    near_sums = dot(spread_v[pl.ds(0, node_dev), :], new_edges_v[...])
    node_first = dot(node_v[...], node_in_v[pl.ds(0, width), :])
    each_peer(lambda peer: arrival(out_sums, in_sums, 2, peer).wait_recv())
    aggregate = (near_sums + dot(back_v[...], in_sums[...])).astype(bf16)
    node_first = node_first + dot(aggregate, node_in_v[pl.ds(width, width), :])
    mixed = dot(half_silu(node_first), node_out_v[...])
    new_nodes_v[...] = residual_norm(node_v[...], mixed).astype(bf16)
    last = pltpu.make_async_copy(new_nodes_v, new_nodes_hbm, store_sem.at[blocks])
    last.start()
    each_peer(lambda peer: transfer(out_rows, in_rows, 0, peer).wait_send())
    each_peer(lambda peer: transfer(out_sums, in_sums, 2, peer).wait_send())

    def finish(block, carry):
        store(block).wait()
        return carry

    lax.fori_loop(0, blocks, finish, 0)
    last.wait()


def shards(
    node_latent,
    edge_latent,
    sender_local,
    receiver_target,
    row_list,
    edge_count,
    edge_in,
    edge_out,
    node_in,
    node_out,
):
    peers = lax.axis_size("space")
    node_dev, width = node_latent.shape
    edge_dev = edge_latent.shape[0]
    capacity = row_list.shape[2]
    pad = -(-capacity // 16) * 16
    listed = row_list.reshape(peers, capacity)
    if pad != capacity:
        listed = jnp.pad(listed, ((0, 0), (0, pad - capacity)), constant_values=-1)
        slot = receiver_target - node_dev
        receiver_target = jnp.where(
            slot < 0, receiver_target, node_dev + slot // capacity * pad + slot % capacity
        )
    slots = peers * pad
    blocks = edge_dev // block_rows
    any_space = pl.BlockSpec(memory_space=pl.ANY)
    index_shape = (edge_dev // lanes, lanes)
    return pl.pallas_call(
        functools.partial(kernel, peers, pad),
        out_shape=(
            jax.ShapeDtypeStruct(node_latent.shape, bf16),
            jax.ShapeDtypeStruct(edge_latent.shape, bf16),
        ),
        in_specs=[pl.BlockSpec(memory_space=pltpu.SMEM)] + [any_space] * 9,
        out_specs=(any_space, any_space),
        scratch_shapes=[
            pltpu.VMEM((node_dev, width), bf16),
            pltpu.VMEM((edge_dev, width), bf16),
            pltpu.VMEM(index_shape, jnp.int32),
            pltpu.VMEM(index_shape, jnp.int32),
            pltpu.VMEM((peers, pad), jnp.int32),
            pltpu.VMEM((width + 2 * node_dev + slots, width), bf16),
            pltpu.VMEM((2 * width, width), bf16),
            pltpu.VMEM((width, width), bf16),
            pltpu.VMEM((2 * width, width), bf16),
            pltpu.VMEM((width, width), bf16),
            pltpu.VMEM((edge_dev, width), f32),
            pltpu.VMEM((edge_dev, slots), bf16),
            pltpu.VMEM((node_dev + slots, edge_dev), bf16),
            pltpu.VMEM((node_dev, slots), bf16),
            pltpu.VMEM((node_dev, width), bf16),
            pltpu.VMEM((edge_dev, width), bf16),
            pltpu.VMEM((slots, width), bf16),
            pltpu.VMEM((slots, width), bf16),
            pltpu.VMEM((slots, width), bf16),
            pltpu.VMEM((slots, width), bf16),
            pltpu.SemaphoreType.DMA((10,)),
            pltpu.SemaphoreType.DMA((blocks + 1,)),
            pltpu.SemaphoreType.DMA((4, peers)),
        ],
        compiler_params=pltpu.CompilerParams(
            collective_id=0, has_side_effects=True, vmem_limit_bytes=56 * 1024 * 1024
        ),
    )(
        edge_count,
        node_latent,
        edge_latent,
        sender_local.reshape(index_shape),
        receiver_target.reshape(index_shape),
        listed,
        edge_in,
        edge_out,
        node_in,
        node_out,
    )


def solution(mesh):
    in_specs = (
        P(("groups", "space"), None),
        P(("groups", "space"), None),
        P("space"),
        P("space"),
        P("space", None, None),
        P("space"),
        P(),
        P(),
        P(),
        P(),
    )
    out_specs = (P(("groups", "space"), None), P(("groups", "space"), None))
    return jax.shard_map(shards, mesh=mesh, in_specs=in_specs, out_specs=out_specs, check_vma=False)
```

```python
import functools

import jax
import jax.numpy as jnp
from jax import lax
from jax.experimental import pallas as pl
from jax.experimental.pallas import tpu as pltpu
from jax.sharding import PartitionSpec as P

epsilon = 1e-05
lanes = 128
block_rows = 256
store_pieces = 4
MESH = pl.DeviceIdType.MESH
bf16 = jnp.bfloat16
f32 = jnp.float32


def dot(left, right):
    return jnp.dot(left, right, preferred_element_type=f32)


def iota(shape, axis):
    return lax.broadcasted_iota(jnp.int32, shape, axis)


def half_silu(first):
    half = 0.5 * first
    return (half + half * jnp.tanh(half)).astype(bf16)


def residual_norm(latent, mixed):
    center = mixed - jnp.mean(mixed, axis=-1, keepdims=True)
    spread = jnp.mean(center * center, axis=-1, keepdims=True)
    return latent.astype(f32) + center * lax.rsqrt(spread + epsilon)


def kernel(
    peers,
    pad,
    count_ref,
    node_hbm,
    edge_hbm,
    send_hbm,
    recv_hbm,
    list_hbm,
    edge_in_hbm,
    edge_out_hbm,
    node_in_hbm,
    node_out_hbm,
    new_edges_v,
    aggregate_v,
    node_first_v,
    node_v,
    node_in_v,
    node_out_v,
    edge_v,
    send_v,
    recv_v,
    list_v,
    table_v,
    ends_v,
    edge_out_v,
    first_v,
    far_hot_v,
    spread_v,
    back_v,
    node_top_v,
    out_rows,
    in_rows,
    out_sums,
    in_sums,
    load_sem,
    sems,
):
    node_dev, width = node_v.shape
    edge_dev = edge_v.shape[0]
    slots = peers * pad
    near = width + 2 * node_dev
    blocks = edge_dev // block_rows
    parts = block_rows // lanes
    me = lax.axis_index("space")

    barrier = pltpu.get_barrier_semaphore()

    def greet(k, carry):
        peer = lax.rem(me + k, peers)
        pl.semaphore_signal(barrier, inc=1, device_id={"space": peer}, device_id_type=MESH)
        return carry

    lax.fori_loop(1, peers, greet, 0)

    loads = [
        pltpu.make_async_copy(source, target, load_sem.at[number])
        for number, (source, target) in enumerate(
            [
                (list_hbm, list_v),
                (node_hbm, node_v),
                (edge_in_hbm.at[pl.ds(width, 2 * width)], ends_v),
                (send_hbm, send_v),
                (recv_hbm, recv_v),
                (edge_in_hbm.at[pl.ds(0, width)], table_v.at[pl.ds(0, width)]),
                (edge_hbm, edge_v),
                (edge_out_hbm, edge_out_v),
                (node_in_hbm.at[pl.ds(0, width)], node_top_v),
                (node_in_hbm.at[pl.ds(width, width)], node_in_v),
                (node_out_hbm, node_out_v),
            ]
        )
    ]
    for load in loads:
        load.start()

    own = pl.ds(pl.multiple_of(me * pad, pad), pad)
    in_rows[own, :] = jnp.zeros((pad, width), bf16)
    in_sums[own, :] = jnp.zeros((pad, width), bf16)

    loads[0].wait()
    listed = list_v[...]
    rows = jnp.concatenate(
        [jnp.broadcast_to(listed[p : p + 1], (pad, pad)) for p in range(peers)], axis=0
    ).astype(f32)
    picked = lax.rem(iota((slots, pad), 0), pad) == iota((slots, pad), 1)
    column = jnp.sum(jnp.where(picked, rows, 0.0), axis=1, keepdims=True)
    wanted = (column.astype(jnp.int32) == iota((slots, node_dev), 1)).astype(f32)
    loads[1].wait()
    out_rows[...] = dot(wanted.astype(bf16), node_v[...]).astype(bf16)

    def transfer(source, target, number, peer):
        theirs = pl.ds(pl.multiple_of(peer * pad, pad), pad)
        return pltpu.make_async_remote_copy(
            src_ref=source.at[theirs],
            dst_ref=target.at[own],
            send_sem=sems.at[number, peer],
            recv_sem=sems.at[number + 1, me],
            device_id={"space": peer},
            device_id_type=MESH,
        )

    def arrival(source, target, number, peer):
        theirs = pl.ds(pl.multiple_of(peer * pad, pad), pad)
        return pltpu.make_async_remote_copy(
            src_ref=source.at[theirs],
            dst_ref=target.at[theirs],
            send_sem=sems.at[number, peer],
            recv_sem=sems.at[number + 1, peer],
            device_id={"space": peer},
            device_id_type=MESH,
        )

    def each_peer(action):
        def step(k, carry):
            action(lax.rem(me + k, peers))
            return carry

        lax.fori_loop(1, peers, step, 0)

    pl.semaphore_wait(barrier, peers - 1)
    each_peer(lambda peer: transfer(out_rows, in_rows, 0, peer).start())

    back_v[...] = wanted.T.astype(bf16)
    loads[2].wait()
    table_v[pl.ds(width, node_dev), :] = dot(node_v[...], ends_v[pl.ds(0, width), :]).astype(bf16)
    table_v[pl.ds(width + node_dev, node_dev), :] = dot(
        node_v[...], ends_v[pl.ds(width, width), :]
    ).astype(bf16)
    for load in loads[3:]:
        load.wait()
    live_count = count_ref[0]

    def columns_of(index_ref, block):
        return jnp.concatenate(
            [
                jnp.broadcast_to(index_ref[pl.ds(block * parts + j, 1), :], (lanes, lanes)).T
                for j in range(parts)
            ],
            axis=0,
        )

    lane_ids = iota((block_rows, lanes), 1)

    def hot(columns, low, high):
        return jnp.concatenate(
            [(columns == lane_ids + c).astype(f32).astype(bf16) for c in range(low, high, lanes)],
            axis=1,
        )

    def before(block, carry):
        here = pl.ds(pl.multiple_of(block * block_rows, block_rows), block_rows)
        senders = columns_of(send_v, block)
        receivers = columns_of(recv_v, block)
        left = jnp.concatenate(
            [edge_v[here, :], hot(senders, 0, node_dev), hot(receivers, 0, node_dev)], axis=1
        )
        first_v[here, :] = dot(left, table_v[pl.ds(0, near), :])
        far_hot_v[here, :] = hot(receivers, node_dev, node_dev + slots)
        for j in range(parts):
            place = block * block_rows + j * lanes
            live = place + iota((1, lanes), 1) < live_count
            target = jnp.where(live, recv_v[pl.ds(block * parts + j, 1), :], -1)
            spread = target == iota((node_dev + slots, lanes), 0)
            spread_v[:, pl.ds(pl.multiple_of(place, lanes), lanes)] = spread.astype(f32).astype(
                bf16
            )
        return carry

    lax.fori_loop(0, blocks, before, 0)

    each_peer(lambda peer: arrival(out_rows, in_rows, 0, peer).wait_recv())
    table_v[pl.ds(near, slots), :] = dot(in_rows[...], ends_v[pl.ds(width, width), :]).astype(bf16)

    def after(block, carry):
        here = pl.ds(pl.multiple_of(block * block_rows, block_rows), block_rows)
        first = first_v[here, :] + dot(far_hot_v[here, :], table_v[pl.ds(near, slots), :])
        mixed = dot(half_silu(first), edge_out_v[...])
        old = edge_v[here, :]
        updated = residual_norm(old, mixed)
        live = block * block_rows + iota((block_rows, 1), 0) < live_count
        new_edges_v[here, :] = jnp.where(live, updated, old.astype(f32)).astype(bf16)
        return carry

    lax.fori_loop(0, blocks, after, 0)

    out_sums[...] = dot(spread_v[pl.ds(node_dev, slots), :], new_edges_v[...]).astype(bf16)
    each_peer(lambda peer: transfer(out_sums, in_sums, 2, peer).start())

    near_sums = dot(spread_v[pl.ds(0, node_dev), :], new_edges_v[...])
    node_first_v[...] = dot(node_v[...], node_top_v[...])
    each_peer(lambda peer: arrival(out_sums, in_sums, 2, peer).wait_recv())
    aggregate_v[...] = (near_sums + dot(back_v[...], in_sums[...])).astype(bf16)
    each_peer(lambda peer: transfer(out_rows, in_rows, 0, peer).wait_send())
    each_peer(lambda peer: transfer(out_sums, in_sums, 2, peer).wait_send())


def finish_kernel(
    edges_v,
    aggregate_v,
    node_first_v,
    node_v,
    node_in_v,
    node_out_v,
    new_nodes_hbm,
    new_edges_hbm,
    new_nodes_v,
    sems,
):
    stores = []
    piece = edges_v.shape[0] // store_pieces
    for number in range(store_pieces):
        here = pl.ds(number * piece, piece)
        stores.append(
            pltpu.make_async_copy(edges_v.at[here], new_edges_hbm.at[here], sems.at[number])
        )
        stores[-1].start()
    node_first = node_first_v[...] + dot(aggregate_v[...], node_in_v[...])
    mixed = dot(half_silu(node_first), node_out_v[...])
    new_nodes_v[...] = residual_norm(node_v[...], mixed).astype(bf16)
    stores.append(pltpu.make_async_copy(new_nodes_v, new_nodes_hbm, sems.at[store_pieces]))
    stores[-1].start()
    for store in stores:
        store.wait()


def shards(
    node_latent,
    edge_latent,
    sender_local,
    receiver_target,
    row_list,
    edge_count,
    edge_in,
    edge_out,
    node_in,
    node_out,
):
    peers = lax.axis_size("space")
    node_dev, width = node_latent.shape
    edge_dev = edge_latent.shape[0]
    capacity = row_list.shape[2]
    pad = -(-capacity // 16) * 16
    listed = row_list.reshape(peers, capacity)
    if pad != capacity:
        listed = jnp.pad(listed, ((0, 0), (0, pad - capacity)), constant_values=-1)
        slot = receiver_target - node_dev
        receiver_target = jnp.where(
            slot < 0, receiver_target, node_dev + slot // capacity * pad + slot % capacity
        )
    slots = peers * pad
    blocks = edge_dev // block_rows
    any_space = pl.BlockSpec(memory_space=pl.ANY)
    index_shape = (edge_dev // lanes, lanes)
    held = pl.pallas_call(
        functools.partial(kernel, peers, pad),
        out_shape=(
            pltpu.VMEM((edge_dev, width), bf16),
            pltpu.VMEM((node_dev, width), bf16),
            pltpu.VMEM((node_dev, width), f32),
            pltpu.VMEM((node_dev, width), bf16),
            pltpu.VMEM((width, width), bf16),
            pltpu.VMEM((width, width), bf16),
        ),
        in_specs=[pl.BlockSpec(memory_space=pltpu.SMEM)] + [any_space] * 9,
        out_specs=[pl.BlockSpec(memory_space=pltpu.VMEM)] * 6,
        scratch_shapes=[
            pltpu.VMEM((edge_dev, width), bf16),
            pltpu.VMEM(index_shape, jnp.int32),
            pltpu.VMEM(index_shape, jnp.int32),
            pltpu.VMEM((peers, pad), jnp.int32),
            pltpu.VMEM((width + 2 * node_dev + slots, width), bf16),
            pltpu.VMEM((2 * width, width), bf16),
            pltpu.VMEM((width, width), bf16),
            pltpu.VMEM((edge_dev, width), f32),
            pltpu.VMEM((edge_dev, slots), bf16),
            pltpu.VMEM((node_dev + slots, edge_dev), bf16),
            pltpu.VMEM((node_dev, slots), bf16),
            pltpu.VMEM((width, width), bf16),
            pltpu.VMEM((slots, width), bf16),
            pltpu.VMEM((slots, width), bf16),
            pltpu.VMEM((slots, width), bf16),
            pltpu.VMEM((slots, width), bf16),
            pltpu.SemaphoreType.DMA((11,)),
            pltpu.SemaphoreType.DMA((4, peers)),
        ],
        compiler_params=pltpu.CompilerParams(
            collective_id=0, has_side_effects=True, vmem_limit_bytes=58 * 1024 * 1024
        ),
    )(
        edge_count,
        node_latent,
        edge_latent,
        sender_local.reshape(index_shape),
        receiver_target.reshape(index_shape),
        listed,
        edge_in,
        edge_out,
        node_in,
        node_out,
    )
    return pl.pallas_call(
        finish_kernel,
        out_shape=(
            jax.ShapeDtypeStruct(node_latent.shape, bf16),
            jax.ShapeDtypeStruct(edge_latent.shape, bf16),
        ),
        in_specs=[pl.BlockSpec(memory_space=pltpu.VMEM)] * 6,
        out_specs=(any_space, any_space),
        scratch_shapes=[
            pltpu.VMEM((node_dev, width), bf16),
            pltpu.SemaphoreType.DMA((store_pieces + 1,)),
        ],
        compiler_params=pltpu.CompilerParams(vmem_limit_bytes=40 * 1024 * 1024),
    )(*held)


def solution(mesh):
    in_specs = (
        P(("groups", "space"), None),
        P(("groups", "space"), None),
        P("space"),
        P("space"),
        P("space", None, None),
        P("space"),
        P(),
        P(),
        P(),
        P(),
    )
    out_specs = (P(("groups", "space"), None), P(("groups", "space"), None))
    return jax.shard_map(shards, mesh=mesh, in_specs=in_specs, out_specs=out_specs, check_vma=False)
```

```python
import functools

import jax
import jax.numpy as jnp
from jax import lax
from jax.experimental import pallas as pl
from jax.experimental.pallas import tpu as pltpu
from jax.sharding import PartitionSpec as P

epsilon = 1e-05
lanes = 128
block_rows = 256
store_pieces = 4
MESH = pl.DeviceIdType.MESH
bf16 = jnp.bfloat16
f32 = jnp.float32


def dot(left, right):
    return jnp.dot(left, right, preferred_element_type=f32)


def iota(shape, axis):
    return lax.broadcasted_iota(jnp.int32, shape, axis)


def half_silu(first):
    half = 0.5 * first
    return (half + half * jnp.tanh(half)).astype(bf16)


def residual_norm(latent, mixed):
    center = mixed - jnp.mean(mixed, axis=-1, keepdims=True)
    spread = jnp.mean(center * center, axis=-1, keepdims=True)
    return latent.astype(f32) + center * lax.rsqrt(spread + epsilon)


def kernel(
    peers,
    pad,
    count_ref,
    node_hbm,
    edge_hbm,
    send_hbm,
    recv_hbm,
    list_hbm,
    edge_in_hbm,
    edge_out_hbm,
    node_in_hbm,
    node_out_hbm,
    new_edges_v,
    aggregate_v,
    node_first_v,
    node_v,
    node_in_v,
    node_out_v,
    edge_v,
    send_v,
    recv_v,
    list_v,
    table_v,
    ends_v,
    edge_out_v,
    first_v,
    far_hot_v,
    spread_v,
    back_v,
    node_top_v,
    out_rows,
    in_rows,
    out_sums,
    in_sums,
    load_sem,
    sems,
):
    node_dev, width = node_v.shape
    edge_dev = edge_v.shape[0]
    slots = peers * pad
    blocks = edge_dev // block_rows
    parts = block_rows // lanes
    me = lax.axis_index("space")

    barrier = pltpu.get_barrier_semaphore()

    def greet(k, carry):
        peer = lax.rem(me + k, peers)
        pl.semaphore_signal(barrier, inc=1, device_id={"space": peer}, device_id_type=MESH)
        return carry

    lax.fori_loop(1, peers, greet, 0)

    loads = [
        pltpu.make_async_copy(source, target, load_sem.at[number])
        for number, (source, target) in enumerate(
            [
                (list_hbm, list_v),
                (node_hbm, node_v),
                (edge_in_hbm.at[pl.ds(width, 2 * width)], ends_v),
                (send_hbm, send_v),
                (recv_hbm, recv_v),
                (edge_in_hbm.at[pl.ds(0, width)], table_v.at[pl.ds(0, width)]),
                (edge_hbm, edge_v),
                (edge_out_hbm, edge_out_v),
                (node_in_hbm.at[pl.ds(0, width)], node_top_v),
                (node_in_hbm.at[pl.ds(width, width)], node_in_v),
                (node_out_hbm, node_out_v),
            ]
        )
    ]
    for load in loads:
        load.start()

    own = pl.ds(pl.multiple_of(me * pad, pad), pad)
    in_rows[own, :] = jnp.zeros((pad, width), bf16)
    in_sums[own, :] = jnp.zeros((pad, width), bf16)

    loads[0].wait()
    listed = list_v[...]
    rows = jnp.concatenate(
        [jnp.broadcast_to(listed[p : p + 1], (pad, pad)) for p in range(peers)], axis=0
    ).astype(f32)
    picked = lax.rem(iota((slots, pad), 0), pad) == iota((slots, pad), 1)
    column = jnp.sum(jnp.where(picked, rows, 0.0), axis=1, keepdims=True)
    wanted = (column.astype(jnp.int32) == iota((slots, node_dev), 1)).astype(f32)
    loads[1].wait()
    loads[2].wait()
    received = dot(node_v[...], ends_v[pl.ds(width, width), :]).astype(bf16)
    table_v[pl.ds(width + node_dev, node_dev), :] = received
    out_rows[...] = dot(wanted.astype(bf16), received).astype(bf16)

    def transfer(source, target, number, peer):
        theirs = pl.ds(pl.multiple_of(peer * pad, pad), pad)
        return pltpu.make_async_remote_copy(
            src_ref=source.at[theirs],
            dst_ref=target.at[own],
            send_sem=sems.at[number, peer],
            recv_sem=sems.at[number + 1, me],
            device_id={"space": peer},
            device_id_type=MESH,
        )

    def arrival(source, target, number, peer):
        theirs = pl.ds(pl.multiple_of(peer * pad, pad), pad)
        return pltpu.make_async_remote_copy(
            src_ref=source.at[theirs],
            dst_ref=target.at[theirs],
            send_sem=sems.at[number, peer],
            recv_sem=sems.at[number + 1, peer],
            device_id={"space": peer},
            device_id_type=MESH,
        )

    def each_peer(action):
        def step(k, carry):
            action(lax.rem(me + k, peers))
            return carry

        lax.fori_loop(1, peers, step, 0)

    pl.semaphore_wait(barrier, peers - 1)
    each_peer(lambda peer: transfer(out_rows, in_rows, 0, peer).start())

    back_v[...] = wanted.T.astype(bf16)
    table_v[pl.ds(width, node_dev), :] = dot(node_v[...], ends_v[pl.ds(0, width), :]).astype(bf16)
    for load in loads[3:]:
        load.wait()
    live_count = count_ref[0]

    def columns_of(index_ref, block):
        return jnp.concatenate(
            [
                jnp.broadcast_to(index_ref[pl.ds(block * parts + j, 1), :], (lanes, lanes)).T
                for j in range(parts)
            ],
            axis=0,
        )

    lane_ids = iota((block_rows, lanes), 1)

    def hot(columns, low, high):
        return jnp.concatenate(
            [(columns == lane_ids + c).astype(f32).astype(bf16) for c in range(low, high, lanes)],
            axis=1,
        )

    def before(block, carry):
        here = pl.ds(pl.multiple_of(block * block_rows, block_rows), block_rows)
        senders = columns_of(send_v, block)
        receivers = columns_of(recv_v, block)
        left = jnp.concatenate(
            [edge_v[here, :], hot(senders, 0, node_dev), hot(receivers, 0, node_dev)], axis=1
        )
        first_v[here, :] = dot(left, table_v[...])
        far_hot_v[here, :] = hot(receivers, node_dev, node_dev + slots)
        for j in range(parts):
            place = block * block_rows + j * lanes
            live = place + iota((1, lanes), 1) < live_count
            target = jnp.where(live, recv_v[pl.ds(block * parts + j, 1), :], -1)
            spread = target == iota((node_dev + slots, lanes), 0)
            spread_v[:, pl.ds(pl.multiple_of(place, lanes), lanes)] = spread.astype(f32).astype(
                bf16
            )
        return carry

    lax.fori_loop(0, blocks, before, 0)

    each_peer(lambda peer: arrival(out_rows, in_rows, 0, peer).wait_recv())

    def after(block, carry):
        here = pl.ds(pl.multiple_of(block * block_rows, block_rows), block_rows)
        first = first_v[here, :] + dot(far_hot_v[here, :], in_rows[...])
        mixed = dot(half_silu(first), edge_out_v[...])
        old = edge_v[here, :]
        updated = residual_norm(old, mixed)
        live = block * block_rows + iota((block_rows, 1), 0) < live_count
        new_edges_v[here, :] = jnp.where(live, updated, old.astype(f32)).astype(bf16)
        return carry

    lax.fori_loop(0, blocks, after, 0, unroll=True)

    out_sums[...] = dot(spread_v[pl.ds(node_dev, slots), :], new_edges_v[...]).astype(bf16)
    each_peer(lambda peer: transfer(out_sums, in_sums, 2, peer).start())

    near_sums = dot(spread_v[pl.ds(0, node_dev), :], new_edges_v[...])
    node_first_v[...] = dot(node_v[...], node_top_v[...])
    each_peer(lambda peer: transfer(out_rows, in_rows, 0, peer).wait_send())
    each_peer(lambda peer: transfer(out_sums, in_sums, 2, peer).wait_send())
    each_peer(lambda peer: arrival(out_sums, in_sums, 2, peer).wait_recv())
    aggregate_v[...] = (near_sums + dot(back_v[...], in_sums[...])).astype(bf16)


def finish_kernel(
    edges_v,
    aggregate_v,
    node_first_v,
    node_v,
    node_in_v,
    node_out_v,
    new_nodes_hbm,
    new_edges_hbm,
    new_nodes_v,
    sems,
):
    stores = []
    piece = edges_v.shape[0] // store_pieces
    for number in range(store_pieces):
        here = pl.ds(number * piece, piece)
        stores.append(
            pltpu.make_async_copy(edges_v.at[here], new_edges_hbm.at[here], sems.at[number])
        )
        stores[-1].start()
    node_first = node_first_v[...] + dot(aggregate_v[...], node_in_v[...])
    mixed = dot(half_silu(node_first), node_out_v[...])
    new_nodes_v[...] = residual_norm(node_v[...], mixed).astype(bf16)
    stores.append(pltpu.make_async_copy(new_nodes_v, new_nodes_hbm, sems.at[store_pieces]))
    stores[-1].start()
    for store in stores:
        store.wait()


def shards(
    node_latent,
    edge_latent,
    sender_local,
    receiver_target,
    row_list,
    edge_count,
    edge_in,
    edge_out,
    node_in,
    node_out,
):
    peers = lax.axis_size("space")
    node_dev, width = node_latent.shape
    edge_dev = edge_latent.shape[0]
    capacity = row_list.shape[2]
    pad = -(-capacity // 16) * 16
    listed = row_list.reshape(peers, capacity)
    if pad != capacity:
        listed = jnp.pad(listed, ((0, 0), (0, pad - capacity)), constant_values=-1)
        slot = receiver_target - node_dev
        receiver_target = jnp.where(
            slot < 0, receiver_target, node_dev + slot // capacity * pad + slot % capacity
        )
    slots = peers * pad
    blocks = edge_dev // block_rows
    any_space = pl.BlockSpec(memory_space=pl.ANY)
    index_shape = (edge_dev // lanes, lanes)
    held = pl.pallas_call(
        functools.partial(kernel, peers, pad),
        out_shape=(
            pltpu.VMEM((edge_dev, width), bf16),
            pltpu.VMEM((node_dev, width), bf16),
            pltpu.VMEM((node_dev, width), f32),
            pltpu.VMEM((node_dev, width), bf16),
            pltpu.VMEM((width, width), bf16),
            pltpu.VMEM((width, width), bf16),
        ),
        in_specs=[pl.BlockSpec(memory_space=pltpu.SMEM)] + [any_space] * 9,
        out_specs=[pl.BlockSpec(memory_space=pltpu.VMEM)] * 6,
        scratch_shapes=[
            pltpu.VMEM((edge_dev, width), bf16),
            pltpu.VMEM(index_shape, jnp.int32),
            pltpu.VMEM(index_shape, jnp.int32),
            pltpu.VMEM((peers, pad), jnp.int32),
            pltpu.VMEM((width + 2 * node_dev, width), bf16),
            pltpu.VMEM((2 * width, width), bf16),
            pltpu.VMEM((width, width), bf16),
            pltpu.VMEM((edge_dev, width), f32),
            pltpu.VMEM((edge_dev, slots), bf16),
            pltpu.VMEM((node_dev + slots, edge_dev), bf16),
            pltpu.VMEM((node_dev, slots), bf16),
            pltpu.VMEM((width, width), bf16),
            pltpu.VMEM((slots, width), bf16),
            pltpu.VMEM((slots, width), bf16),
            pltpu.VMEM((slots, width), bf16),
            pltpu.VMEM((slots, width), bf16),
            pltpu.SemaphoreType.DMA((11,)),
            pltpu.SemaphoreType.DMA((4, peers)),
        ],
        compiler_params=pltpu.CompilerParams(
            collective_id=0, has_side_effects=True, vmem_limit_bytes=58 * 1024 * 1024
        ),
    )(
        edge_count,
        node_latent,
        edge_latent,
        sender_local.reshape(index_shape),
        receiver_target.reshape(index_shape),
        listed,
        edge_in,
        edge_out,
        node_in,
        node_out,
    )
    return pl.pallas_call(
        finish_kernel,
        out_shape=(
            jax.ShapeDtypeStruct(node_latent.shape, bf16),
            jax.ShapeDtypeStruct(edge_latent.shape, bf16),
        ),
        in_specs=[pl.BlockSpec(memory_space=pltpu.VMEM)] * 6,
        out_specs=(any_space, any_space),
        scratch_shapes=[
            pltpu.VMEM((node_dev, width), bf16),
            pltpu.SemaphoreType.DMA((store_pieces + 1,)),
        ],
        compiler_params=pltpu.CompilerParams(vmem_limit_bytes=40 * 1024 * 1024),
    )(*held)


def solution(mesh):
    in_specs = (
        P(("groups", "space"), None),
        P(("groups", "space"), None),
        P("space"),
        P("space"),
        P("space", None, None),
        P("space"),
        P(),
        P(),
        P(),
        P(),
    )
    out_specs = (P(("groups", "space"), None), P(("groups", "space"), None))
    return jax.shard_map(shards, mesh=mesh, in_specs=in_specs, out_specs=out_specs, check_vma=False)
```

```python
import functools

import jax
import jax.numpy as jnp
from jax import lax
from jax.experimental import pallas as pl
from jax.experimental.pallas import tpu as pltpu
from jax.sharding import PartitionSpec as P

epsilon = 1e-05
lanes = 128
block_rows = 256
store_pieces = 4
MESH = pl.DeviceIdType.MESH
bf16 = jnp.bfloat16
f32 = jnp.float32


def dot(left, right):
    return jnp.dot(left, right, preferred_element_type=f32)


def iota(shape, axis):
    return lax.broadcasted_iota(jnp.int32, shape, axis)


def half_silu(first):
    half = 0.5 * first
    return (half + half * jnp.tanh(half)).astype(bf16)


def residual_norm(latent, mixed):
    center = mixed - jnp.mean(mixed, axis=-1, keepdims=True)
    spread = jnp.mean(center * center, axis=-1, keepdims=True)
    return latent.astype(f32) + center * lax.rsqrt(spread + epsilon)


def kernel(
    peers,
    pad,
    count_ref,
    node_hbm,
    edge_hbm,
    send_hbm,
    recv_hbm,
    list_hbm,
    edge_in_hbm,
    edge_out_hbm,
    node_in_hbm,
    node_out_hbm,
    new_edges_v,
    aggregate_v,
    node_first_v,
    node_v,
    node_in_v,
    node_out_v,
    edge_v,
    send_v,
    recv_v,
    list_v,
    table_v,
    ends_v,
    edge_out_v,
    first_v,
    far_hot_v,
    spread_v,
    back_v,
    node_top_v,
    out_rows,
    in_rows,
    out_sums,
    in_sums,
    load_sem,
    sems,
):
    node_dev, width = node_v.shape
    edge_dev = edge_v.shape[0]
    slots = peers * pad
    blocks = edge_dev // block_rows
    parts = block_rows // lanes
    me = lax.axis_index("space")

    barrier = pltpu.get_barrier_semaphore()

    def greet(k, carry):
        peer = lax.rem(me + k, peers)
        pl.semaphore_signal(barrier, inc=1, device_id={"space": peer}, device_id_type=MESH)
        return carry

    lax.fori_loop(1, peers, greet, 0)

    loads = [
        pltpu.make_async_copy(source, target, load_sem.at[number])
        for number, (source, target) in enumerate(
            [
                (list_hbm, list_v),
                (node_hbm, node_v),
                (edge_in_hbm.at[pl.ds(width, 2 * width)], ends_v),
                (send_hbm, send_v),
                (recv_hbm, recv_v),
                (edge_in_hbm.at[pl.ds(0, width)], table_v.at[pl.ds(0, width)]),
                (edge_hbm, edge_v),
                (edge_out_hbm, edge_out_v),
                (node_in_hbm.at[pl.ds(0, width)], node_top_v),
                (node_in_hbm.at[pl.ds(width, width)], node_in_v),
                (node_out_hbm, node_out_v),
            ]
        )
    ]
    for load in loads:
        load.start()

    own = pl.ds(pl.multiple_of(me * pad, pad), pad)
    in_rows[own, :] = jnp.zeros((pad, width), bf16)
    in_sums[own, :] = jnp.zeros((pad, width), bf16)

    loads[0].wait()
    listed = list_v[...]
    rows = jnp.concatenate(
        [jnp.broadcast_to(listed[p : p + 1], (pad, pad)) for p in range(peers)], axis=0
    ).astype(f32)
    picked = lax.rem(iota((slots, pad), 0), pad) == iota((slots, pad), 1)
    column = jnp.sum(jnp.where(picked, rows, 0.0), axis=1, keepdims=True)
    wanted = (column.astype(jnp.int32) == iota((slots, node_dev), 1)).astype(f32)
    loads[1].wait()
    loads[2].wait()
    received = dot(node_v[...], ends_v[pl.ds(width, width), :]).astype(bf16)
    table_v[pl.ds(width + node_dev, node_dev), :] = received
    out_rows[...] = dot(wanted.astype(bf16), received).astype(bf16)

    def transfer(source, target, number, peer):
        theirs = pl.ds(pl.multiple_of(peer * pad, pad), pad)
        return pltpu.make_async_remote_copy(
            src_ref=source.at[theirs],
            dst_ref=target.at[own],
            send_sem=sems.at[number, peer],
            recv_sem=sems.at[number + 1, me],
            device_id={"space": peer},
            device_id_type=MESH,
        )

    def arrival(source, target, number, peer):
        theirs = pl.ds(pl.multiple_of(peer * pad, pad), pad)
        return pltpu.make_async_remote_copy(
            src_ref=source.at[theirs],
            dst_ref=target.at[theirs],
            send_sem=sems.at[number, peer],
            recv_sem=sems.at[number + 1, peer],
            device_id={"space": peer},
            device_id_type=MESH,
        )

    def each_peer(action):
        def step(k, carry):
            action(lax.rem(me + k, peers))
            return carry

        lax.fori_loop(1, peers, step, 0)

    pl.semaphore_wait(barrier, peers - 1)
    each_peer(lambda peer: transfer(out_rows, in_rows, 0, peer).start())

    back_v[...] = wanted.T.astype(bf16)
    table_v[pl.ds(width, node_dev), :] = dot(node_v[...], ends_v[pl.ds(0, width), :]).astype(bf16)
    for load in loads[3:]:
        load.wait()
    live_count = count_ref[0]

    def columns_of(index_ref, block):
        return jnp.concatenate(
            [
                jnp.broadcast_to(index_ref[pl.ds(block * parts + j, 1), :], (lanes, lanes)).T
                for j in range(parts)
            ],
            axis=0,
        )

    lane_ids = iota((block_rows, lanes), 1)

    def hot(columns, low, high):
        return jnp.concatenate(
            [(columns == lane_ids + c).astype(f32).astype(bf16) for c in range(low, high, lanes)],
            axis=1,
        )

    def before(block, carry):
        here = pl.ds(pl.multiple_of(block * block_rows, block_rows), block_rows)
        senders = columns_of(send_v, block)
        receivers = columns_of(recv_v, block)
        left = jnp.concatenate(
            [edge_v[here, :], hot(senders, 0, node_dev), hot(receivers, 0, node_dev)], axis=1
        )
        first_v[here, :] = dot(left, table_v[...])
        far_hot_v[here, :] = hot(receivers, node_dev, node_dev + slots)
        for j in range(parts):
            place = block * block_rows + j * lanes
            live = place + iota((1, lanes), 1) < live_count
            target = jnp.where(live, recv_v[pl.ds(block * parts + j, 1), :], -1)
            spread = target == iota((node_dev + slots, lanes), 0)
            spread_v[:, pl.ds(pl.multiple_of(place, lanes), lanes)] = spread.astype(f32).astype(
                bf16
            )
        return carry

    lax.fori_loop(0, blocks, before, 0, unroll=2)

    each_peer(lambda peer: arrival(out_rows, in_rows, 0, peer).wait_recv())

    def after(block, sums):
        here = pl.ds(pl.multiple_of(block * block_rows, block_rows), block_rows)
        first = first_v[here, :] + dot(far_hot_v[here, :], in_rows[...])
        mixed = dot(half_silu(first), edge_out_v[...])
        old = edge_v[here, :]
        updated = residual_norm(old, mixed)
        live = block * block_rows + iota((block_rows, 1), 0) < live_count
        kept = jnp.where(live, updated, old.astype(f32)).astype(bf16)
        new_edges_v[here, :] = kept
        return sums + dot(spread_v[pl.ds(node_dev, slots), here], kept)

    far_sums = lax.fori_loop(0, blocks, after, jnp.zeros((slots, width), f32), unroll=True)
    out_sums[...] = far_sums.astype(bf16)
    each_peer(lambda peer: transfer(out_sums, in_sums, 2, peer).start())

    near_sums = dot(spread_v[pl.ds(0, node_dev), :], new_edges_v[...])
    node_first_v[...] = dot(node_v[...], node_top_v[...])
    each_peer(lambda peer: transfer(out_rows, in_rows, 0, peer).wait_send())
    each_peer(lambda peer: transfer(out_sums, in_sums, 2, peer).wait_send())
    each_peer(lambda peer: arrival(out_sums, in_sums, 2, peer).wait_recv())
    aggregate_v[...] = (near_sums + dot(back_v[...], in_sums[...])).astype(bf16)


def finish_kernel(
    edges_v,
    aggregate_v,
    node_first_v,
    node_v,
    node_in_v,
    node_out_v,
    new_nodes_hbm,
    new_edges_hbm,
    new_nodes_v,
    sems,
):
    stores = []
    piece = edges_v.shape[0] // store_pieces
    for number in range(store_pieces):
        here = pl.ds(number * piece, piece)
        stores.append(
            pltpu.make_async_copy(edges_v.at[here], new_edges_hbm.at[here], sems.at[number])
        )
        stores[-1].start()
    node_first = node_first_v[...] + dot(aggregate_v[...], node_in_v[...])
    mixed = dot(half_silu(node_first), node_out_v[...])
    new_nodes_v[...] = residual_norm(node_v[...], mixed).astype(bf16)
    stores.append(pltpu.make_async_copy(new_nodes_v, new_nodes_hbm, sems.at[store_pieces]))
    stores[-1].start()
    for store in stores:
        store.wait()


def shards(
    node_latent,
    edge_latent,
    sender_local,
    receiver_target,
    row_list,
    edge_count,
    edge_in,
    edge_out,
    node_in,
    node_out,
):
    peers = lax.axis_size("space")
    node_dev, width = node_latent.shape
    edge_dev = edge_latent.shape[0]
    capacity = row_list.shape[2]
    pad = -(-capacity // 16) * 16
    listed = row_list.reshape(peers, capacity)
    if pad != capacity:
        listed = jnp.pad(listed, ((0, 0), (0, pad - capacity)), constant_values=-1)
        slot = receiver_target - node_dev
        receiver_target = jnp.where(
            slot < 0, receiver_target, node_dev + slot // capacity * pad + slot % capacity
        )
    slots = peers * pad
    blocks = edge_dev // block_rows
    any_space = pl.BlockSpec(memory_space=pl.ANY)
    index_shape = (edge_dev // lanes, lanes)
    held = pl.pallas_call(
        functools.partial(kernel, peers, pad),
        out_shape=(
            pltpu.VMEM((edge_dev, width), bf16),
            pltpu.VMEM((node_dev, width), bf16),
            pltpu.VMEM((node_dev, width), f32),
            pltpu.VMEM((node_dev, width), bf16),
            pltpu.VMEM((width, width), bf16),
            pltpu.VMEM((width, width), bf16),
        ),
        in_specs=[pl.BlockSpec(memory_space=pltpu.SMEM)] + [any_space] * 9,
        out_specs=[pl.BlockSpec(memory_space=pltpu.VMEM)] * 6,
        scratch_shapes=[
            pltpu.VMEM((edge_dev, width), bf16),
            pltpu.VMEM(index_shape, jnp.int32),
            pltpu.VMEM(index_shape, jnp.int32),
            pltpu.VMEM((peers, pad), jnp.int32),
            pltpu.VMEM((width + 2 * node_dev, width), bf16),
            pltpu.VMEM((2 * width, width), bf16),
            pltpu.VMEM((width, width), bf16),
            pltpu.VMEM((edge_dev, width), f32),
            pltpu.VMEM((edge_dev, slots), bf16),
            pltpu.VMEM((node_dev + slots, edge_dev), bf16),
            pltpu.VMEM((node_dev, slots), bf16),
            pltpu.VMEM((width, width), bf16),
            pltpu.VMEM((slots, width), bf16),
            pltpu.VMEM((slots, width), bf16),
            pltpu.VMEM((slots, width), bf16),
            pltpu.VMEM((slots, width), bf16),
            pltpu.SemaphoreType.DMA((11,)),
            pltpu.SemaphoreType.DMA((4, peers)),
        ],
        compiler_params=pltpu.CompilerParams(
            collective_id=0, has_side_effects=True, vmem_limit_bytes=58 * 1024 * 1024
        ),
    )(
        edge_count,
        node_latent,
        edge_latent,
        sender_local.reshape(index_shape),
        receiver_target.reshape(index_shape),
        listed,
        edge_in,
        edge_out,
        node_in,
        node_out,
    )
    return pl.pallas_call(
        finish_kernel,
        out_shape=(
            jax.ShapeDtypeStruct(node_latent.shape, bf16),
            jax.ShapeDtypeStruct(edge_latent.shape, bf16),
        ),
        in_specs=[pl.BlockSpec(memory_space=pltpu.VMEM)] * 6,
        out_specs=(any_space, any_space),
        scratch_shapes=[
            pltpu.VMEM((node_dev, width), bf16),
            pltpu.SemaphoreType.DMA((store_pieces + 1,)),
        ],
        compiler_params=pltpu.CompilerParams(vmem_limit_bytes=40 * 1024 * 1024),
    )(*held)


def solution(mesh):
    in_specs = (
        P(("groups", "space"), None),
        P(("groups", "space"), None),
        P("space"),
        P("space"),
        P("space", None, None),
        P("space"),
        P(),
        P(),
        P(),
        P(),
    )
    out_specs = (P(("groups", "space"), None), P(("groups", "space"), None))
    return jax.shard_map(shards, mesh=mesh, in_specs=in_specs, out_specs=out_specs, check_vma=False)
```
